32 devices in a mesh: gx: 4 (over y, x), yz: 8 (over z, core).
Axes of the slice: x: 2, y: 2, z: 4, core: 2. Of those that a mesh axis runs over, the one named last changes fastest.
Arguments:
- seg_ends: float32 [6, 131072], P(None, ('gx', 'yz')), may hold values from -6 to 6
- burgers: float32 [3, 131072], P(None, ('gx', 'yz')), may hold values from -6 to 6
- cell_index: int32 [131072], P(('gx', 'yz')), may hold values from 0 to 1023
- send_list: int32 [4, 4096], P(None, ('gx', 'yz')), may hold values from -1 to 4095, as said below
- pair_list: int32 [2, 8192], P(None, ('gx', 'yz')), may hold values from -1 to 35, as said below
- coupling: float32 [6, 9], replicated, may hold values from -2 to 2
Outputs:
- forces: float32 [3, 131072], P(None, ('gx', 'yz'))
The draws below stay inside these ranges and needn't reach their ends.
Inputs may be any that keep to these rules, and one draw needn't show every extreme that they name: `send_list`: per domain and neighbour, up to 128 distinct rows of 0 to 4095 come first, then -1 in the remaining slots; some list in every draw is full. `pair_list`: per domain, target t < 32 and t <= s < 36, no pair twice; empty slots are -1 in both rows and follow the used ones; some domain fills all 256 slots in every draw.
All inputs are finite; a program needn't handle non-finite values.
Results may differ from the reference program's by a relative error of at most 0.0003.
Values sent between devices are 32-bit elements; how exact they have to be, the bound alone decides.
A program may use at most 64 MiB of HBM per device.

```python
import jax
import jax.numpy as jnp
from jax import lax

G = 32
S_DEV = 4096
TILE = 128
NPAIR = 256
PAIR_BLOCK = 16
OWN = 1024
SEGS = 131072
N_GX = 4
N_YZ = 8


def draw_send_list(key, part):
    key = jax.random.fold_in(key, 11)
    domains = SEGS // S_DEV
    choose_key, count_key = jax.random.split(key)
    row_keys = jax.random.split(choose_key, domains * 4)

    def first_rows(one_key):
        return jax.random.permutation(one_key, S_DEV)[:TILE]
    chosen = jax.vmap(first_rows)(row_keys).reshape(domains, 4, TILE)
    counts = jax.random.randint(count_key, (domains, 4), TILE // 2, TILE + 1)
    counts = counts.at[0, 0].set(TILE)
    slot_ids = jnp.arange(TILE)
    padded = jnp.where(slot_ids[None, None, :] < counts[:, :, None], chosen, -1)
    return jnp.transpose(padded, (1, 0, 2)).reshape(4, domains * TILE).astype(jnp.int32)


def draw_pair_list(key, part):
    key = jax.random.fold_in(key, 12)
    domains = SEGS // S_DEV
    local_tiles = S_DEV // TILE
    all_tiles = local_tiles + 4
    candidates = local_tiles * all_tiles
    score_key, count_key = jax.random.split(key)
    row_keys = jax.random.split(score_key, domains)
    grid_ids = jnp.arange(candidates)
    allowed = grid_ids % all_tiles >= grid_ids // all_tiles

    def choose(one_key):
        scores = jax.random.permutation(one_key, candidates)
        scores = jnp.where(allowed, scores, scores + candidates)
        return jnp.argsort(scores, stable=True)[:NPAIR]
    chosen = jax.vmap(choose)(row_keys)
    counts = jax.random.randint(count_key, (domains,), max(NPAIR // 8, 1), NPAIR + 1)
    counts = counts.at[0].set(NPAIR)
    live = jnp.arange(NPAIR)[None, :] < counts[:, None]
    targets = jnp.where(live, chosen // all_tiles, -1)
    sources = jnp.where(live, chosen % all_tiles, -1)
    return jnp.stack([targets.reshape(-1), sources.reshape(-1)]).astype(jnp.int32)


def with_ends(result, own_key, low, high):
    extent = result.shape
    spot = [jax.random.randint(jax.random.fold_in(own_key, axis), (), 0, extent[axis]) for axis in range(len(extent))]
    result = result.at[tuple(spot)].set(low)
    longest = extent.index(max(extent))
    spot[longest] = (spot[longest] + 1) % extent[longest]
    return result.at[tuple(spot)].set(high)


def steps_of(key, dims, cuts, least, largest):
    gain, own = 1.0, jax.random.fold_in(key, 6)
    for dim, shards_of in cuts:
        draws = jnp.exp(jax.random.uniform(jax.random.fold_in(own, dim), (shards_of,), jnp.float32, least / len(cuts), largest / len(cuts)))
        gain = gain * jnp.repeat(draws, dims[dim] // shards_of).reshape([-1 if axis == dim else 1 for axis in range(len(dims))])
    return gain


def centred(rng, dims, deviation, most, cuts=(), held_as=jnp.bfloat16):
    array = deviation * jax.random.normal(rng, dims, jnp.float32)
    if cuts:
        array = array * steps_of(rng, dims, cuts, -0.22, 0.18)
    return jnp.clip(array, -most, most).astype(held_as)


def setup_inputs(seed: int = 0) -> dict:
    streams_of = jax.random.split(jax.random.key(seed), 7)
    return {
        "seg_ends": centred(streams_of[0], (6, SEGS), 1.0, 6.0, ((1, 32),), jnp.float32),
        "burgers": centred(streams_of[1], (3, SEGS), 1.0, 6.0, ((1, 32),), jnp.float32),
        "cell_index": with_ends(jax.random.randint(streams_of[2], (SEGS,), 0, OWN), jax.random.fold_in(streams_of[2], 1), 0, OWN - 1).astype(jnp.int32),
        "send_list": draw_send_list(jax.random.fold_in(streams_of[6], 71), 0),
        "pair_list": draw_pair_list(jax.random.fold_in(streams_of[6], 71), 0),
        "coupling": centred(streams_of[5], (6, 9), 9 ** -0.5, 2.0, (), jnp.float32),
    }


far_scale = 0.003
near_scale = 0.25
core_square = 1.0
kernel_spread = 4.0

def kernel_rows(first_row, row_count, width):
    rows = first_row + jnp.arange(row_count, dtype=jnp.int32)
    columns = jnp.arange(width, dtype=jnp.int32)
    apart = jnp.abs(rows[:, None] - columns[None, :])
    apart = jnp.minimum(apart, width - apart).astype(jnp.float32)
    return 1.0 / (1.0 + (apart / kernel_spread) ** 2)

def peach_koehler(stress, burgers, tangent):
    push_x = stress[0] * burgers[0] + stress[5] * burgers[1] + stress[4] * burgers[2]
    push_y = stress[5] * burgers[0] + stress[1] * burgers[1] + stress[3] * burgers[2]
    push_z = stress[4] * burgers[0] + stress[3] * burgers[1] + stress[2] * burgers[2]
    return jnp.stack([push_y * tangent[2] - push_z * tangent[1], push_z * tangent[0] - push_x * tangent[2], push_x * tangent[1] - push_y * tangent[0]])

def pair_block(tiles, targets, sources):
    tile_count = tiles.shape[0]
    usable = targets >= 0
    target_safe = jnp.maximum(targets, 0)
    source_safe = jnp.maximum(sources, 0)
    target_rows = tiles[target_safe]
    source_rows = tiles[source_safe]
    target_mid = 0.5 * (target_rows[:, 0:3] + target_rows[:, 3:6])
    source_mid = 0.5 * (source_rows[:, 0:3] + source_rows[:, 3:6])
    offset = target_mid[:, :, :, None] - source_mid[:, :, None, :]
    distance = core_square + lax.optimization_barrier(jnp.sum(offset * offset, axis=1))
    intersection = lax.optimization_barrier(jnp.sum(target_rows[:, 6:9, :, None] * source_rows[:, 6:9, None, :], axis=1))
    weight = near_scale * intersection / (distance * jnp.sqrt(distance))
    weight = weight * usable[:, None, None].astype(jnp.float32)
    pushed = weight[:, None] * offset
    on_target = lax.optimization_barrier(jnp.sum(pushed, axis=3))
    distinct = (targets != sources).astype(jnp.float32)
    on_source = -lax.optimization_barrier(jnp.sum(pushed, axis=2)) * distinct[:, None, None]
    tile_ids = jnp.arange(tile_count, dtype=jnp.int32)
    target_hot = (target_safe[:, None] == tile_ids[None, :]).astype(jnp.float32)
    source_hot = (source_safe[:, None] == tile_ids[None, :]).astype(jnp.float32)
    high = lax.Precision.HIGHEST
    return jnp.einsum('pn,pct->nct', target_hot, on_target, precision=high) + jnp.einsum('pn,pct->nct', source_hot, on_source, precision=high)

def reference(seg_ends, burgers, cell_index, send_list, pair_list, coupling):
    high = lax.Precision.HIGHEST
    domains = N_GX * N_YZ
    span_x = G // N_GX
    span_y = G // N_YZ
    local_tiles = S_DEV // TILE
    tangent = seg_ends[3:6] - seg_ends[0:3]
    moment_terms = (burgers[:, None, :] * tangent[None, :, :]).reshape(9, SEGS)
    seg_ids = jnp.arange(SEGS, dtype=jnp.int32)
    owner = seg_ids // S_DEV
    cell_x = owner // N_YZ * span_x + cell_index // (span_y * G)
    cell_y = owner % N_YZ * span_y + cell_index // G % span_y
    cell_z = cell_index % G
    flat_cell = ((cell_x * G + cell_y) * G + cell_z).astype(jnp.int32)
    grid = jax.ops.segment_sum(moment_terms.T, flat_cell, num_segments=G * G * G).T.reshape(9, G, G, G)
    kernel = kernel_rows(0, G, G)
    along_x = jnp.einsum('xa,kabc->kxbc', kernel, grid, precision=high)
    along_y = jnp.einsum('yb,kxbc->kxyc', kernel, along_x, precision=high)
    along_z = jnp.einsum('zc,kxyc->kxyz', kernel, along_y, precision=high)
    stress = far_scale * jnp.dot(coupling, along_z.reshape(9, G * G * G), precision=high)
    far_force = peach_koehler(jnp.take(stress, flat_cell, axis=1), burgers, tangent)
    segment_data = jnp.concatenate([seg_ends, burgers], axis=0)
    lists = send_list.reshape(4, domains, TILE)
    pairs = pair_list.reshape(2, domains, NPAIR)

    def senders(domain):
        slab = domain // N_YZ
        column = domain % N_YZ
        return jnp.stack([(slab - 1) % N_GX * N_YZ + column, (slab + 1) % N_GX * N_YZ + column, slab * N_YZ + (column - 1) % N_YZ, slab * N_YZ + (column + 1) % N_YZ]).astype(jnp.int32)

    def one_domain(domain):
        owned_rows = lax.dynamic_slice_in_dim(segment_data, domain * S_DEV, S_DEV, 1)
        local_blocks = owned_rows.reshape(9, local_tiles, TILE).transpose(1, 0, 2)
        source_ids = senders(domain)
        ghost_rows = []
        for neighbour in range(4):
            sender = source_ids[neighbour]
            picked = lists[neighbour][sender]
            usable = (picked >= 0).astype(jnp.float32)
            rows = jnp.take(segment_data, sender * S_DEV + jnp.maximum(picked, 0), axis=1)
            ghost_rows.append(rows * usable[None, :])
        tiles = jnp.concatenate([local_blocks, jnp.stack(ghost_rows)], axis=0)
        domain_pairs = pairs[:, domain]

        def accumulate(block_index, totals):
            targets = lax.dynamic_slice_in_dim(domain_pairs[0], block_index * PAIR_BLOCK, PAIR_BLOCK)
            sources = lax.dynamic_slice_in_dim(domain_pairs[1], block_index * PAIR_BLOCK, PAIR_BLOCK)
            return totals + pair_block(tiles, targets, sources)
        empty = jnp.zeros((local_tiles + 4, 3, TILE), jnp.float32)
        return lax.fori_loop(0, NPAIR // PAIR_BLOCK, accumulate, empty)
    domain_ids = jnp.arange(domains, dtype=jnp.int32)
    totals = lax.map(one_domain, domain_ids)
    near_force = totals[:, :local_tiles].transpose(2, 0, 1, 3).reshape(3, SEGS)
    forces = far_force + near_force
    source_all = jax.vmap(senders)(domain_ids)
    for neighbour in range(4):
        sender = source_all[:, neighbour]
        picked = lists[neighbour][sender]
        target = jnp.where(picked >= 0, sender[:, None] * S_DEV + picked, SEGS).astype(jnp.int32)
        returned = totals[:, local_tiles + neighbour].transpose(1, 0, 2).reshape(3, domains * TILE)
        forces = forces.at[:, target.reshape(-1)].add(returned, mode='drop')
    return forces
```

```python
import functools

import jax
import jax.numpy as jnp
import numpy as np
from jax import lax
from jax.experimental import pallas as pl
from jax.experimental.pallas import tpu as pltpu
from jax.sharding import PartitionSpec as P

G = 32
TILE = 128
LANES = 128
TOGETHER = 8
CHUNK = 512

far_scale = 0.003
near_scale = 0.25
core_square = 1.0
kernel_spread = 4.0

MESH = pl.DeviceIdType.MESH
f32 = jnp.float32
bf16 = jnp.bfloat16
NT = (((1,), (1,)), ((), ()))
NN = (((1,), (0,)), ((), ()))


def kernel_of(apart):
    apart = np.abs(apart) % G
    apart = np.minimum(apart, G - apart).astype(np.float32)
    return (1.0 / (1.0 + (apart / np.float32(kernel_spread)) ** 2)).astype(np.float32)


def column_matrices(column_count, span_y):
    cells = span_y * G
    width = -(-cells // LANES) * LANES
    at = np.arange(cells)
    result = np.zeros((column_count, width, width), np.float32)
    for slot in range(column_count):
        from_y = slot * span_y + at // G
        result[slot, :cells, :cells] = kernel_of(from_y[:, None] - (at // G)[None, :]) * kernel_of(
            (at % G)[:, None] - (at % G)[None, :]
        )
    return result


def slab_matrices(slab_count, span_x):
    at = np.arange(span_x)
    result = []
    for slot in range(slab_count):
        along = kernel_of((slot * span_x + at)[None, :] - at[:, None]) * np.float32(far_scale)
        result.append(np.kron(along, np.eye(8, dtype=np.float32)))
    return np.stack(result).astype(np.float32)


def pieces_of(x):
    first = x.astype(bf16).astype(f32)
    rest = x - first
    second = rest.astype(bf16).astype(f32)
    return first, second, rest - second


def dot(a, b, dims=NN):
    return lax.dot_general(a, b, dims, preferred_element_type=f32)


def dot_high(a, b):
    return lax.dot_general(a, b, NN, precision=lax.Precision.HIGHEST, preferred_element_type=f32)


def body(
    span_x,
    span_y,
    slab_count,
    column_count,
    seg_ref,
    burgers_ref,
    cell_ref,
    send_ref,
    pair_ref,
    pair_smem,
    coupling_ref,
    column_ref,
    slab_ref,
    out_ref,
    raw,
    ghost_out,
    ghost_in,
    left_ops,
    right_ops,
    mid_ops,
    hot_cells,
    moments,
    column_slots,
    slab_slots,
    stress,
    pushed,
    return_out,
    return_in,
    ghost_send,
    ghost_recv,
    column_send,
    column_recv,
    slab_send,
    slab_recv,
    return_send,
    return_recv,
):
    seg_count = seg_ref.shape[1]
    local_tiles = seg_count // TILE
    pair_count = pair_ref.shape[1]
    cells = span_y * G
    width = column_ref.shape[1]
    gx = lax.axis_index("gx")
    yz = lax.axis_index("yz")

    def slab_peer(by):
        return (lax.rem(gx + by, slab_count), yz)

    def column_peer(by):
        return (gx, lax.rem(yz + by, column_count))

    barrier = pltpu.get_barrier_semaphore()
    for by in range(1, slab_count):
        pl.semaphore_signal(barrier, inc=1, device_id=slab_peer(by), device_id_type=MESH)
    for by in range(1, column_count):
        pl.semaphore_signal(barrier, inc=1, device_id=column_peer(by), device_id_type=MESH)

    raw[...] = jnp.zeros_like(raw)
    for tile in range(local_tiles):
        at = slice(tile * TILE, (tile + 1) * TILE)
        raw[tile, 0:3] = 0.5 * (seg_ref[0:3, at] + seg_ref[3:6, at])
        raw[tile, 8:11] = burgers_ref[0:3, at]

    sub = lax.broadcasted_iota(jnp.int32, (TILE, 4 * TILE), 0)
    rows = jnp.concatenate([send_ref[n : n + 1, :] for n in range(4)], axis=1)
    row_tile = rows >> 7
    hot_rows = jnp.where(sub == (rows & 127), 1.0, 0.0).astype(bf16)
    flat = raw[0:local_tiles].reshape(local_tiles * 16, TILE)
    first, second, third = (piece.astype(bf16) for piece in pieces_of(flat))
    picked = dot(first, hot_rows) + dot(second, hot_rows) + dot(third, hot_rows)
    outgoing = jnp.zeros((16, 4 * TILE), f32)
    for tile in range(local_tiles):
        outgoing = outgoing + jnp.where(row_tile == tile, picked[tile * 16 : (tile + 1) * 16], 0.0)
    for n in range(4):
        ghost_out[n] = outgoing[:, n * TILE : (n + 1) * TILE]

    pl.semaphore_wait(barrier, slab_count - 1 + column_count - 1)

    onward = [
        slab_peer(1),
        slab_peer(slab_count - 1),
        column_peer(1),
        column_peer(column_count - 1),
    ]
    backward = [onward[1], onward[0], onward[3], onward[2]]
    ghost_copies = []
    for n in range(4):
        copy = pltpu.make_async_remote_copy(
            src_ref=ghost_out.at[n],
            dst_ref=ghost_in.at[n],
            send_sem=ghost_send.at[n],
            recv_sem=ghost_recv.at[n],
            device_id=onward[n],
            device_id_type=MESH,
        )
        copy.start()
        ghost_copies.append(copy)

    moments[...] = jnp.zeros_like(moments)

    @pl.loop(0, seg_count // CHUNK)
    def _(step):
        at = pl.ds(pl.multiple_of(step * CHUNK, CHUNK), CHUNK)
        cell = cell_ref[:, at]
        high = cell // cells
        low = cell - high * cells
        hot = jnp.where(lax.broadcasted_iota(jnp.int32, (width, CHUNK), 0) == low, 1.0, 0.0).astype(bf16)
        hot_cells[:, at] = hot
        tangent = seg_ref[3:6, at] - seg_ref[0:3, at]
        vector = burgers_ref[:, at]
        terms = jnp.concatenate(
            [vector[a : a + 1] * tangent for a in range(3)] + [jnp.zeros((7, CHUNK), f32)], axis=0
        )
        stacked = []
        for piece in pieces_of(terms):
            for x in range(span_x):
                stacked.append(jnp.where(high == x, piece, 0.0).astype(bf16))
        moments[...] += dot(jnp.concatenate(stacked, axis=0), hot, NT)

    count = span_x * 16
    summed = moments[0:count] + moments[count : 2 * count] + moments[2 * count : 3 * count]
    column_slots[0] = jnp.zeros_like(column_slots[0])
    for x in range(span_x):
        total = jnp.zeros((6, width), f32)
        for k in range(9):
            total = total + coupling_ref[:, k : k + 1] * summed[x * 16 + k : x * 16 + k + 1]
        column_slots[0, x * 8 : x * 8 + 6] = total

    column_copies = []
    for by in range(1, column_count):
        copy = pltpu.make_async_remote_copy(
            src_ref=column_slots.at[0],
            dst_ref=column_slots.at[column_count - by],
            send_sem=column_send.at[by],
            recv_sem=column_recv.at[column_count - by],
            device_id=column_peer(by),
            device_id_type=MESH,
        )
        copy.start()
        column_copies.append(copy)

    eight = lax.broadcasted_iota(jnp.int32, (8, TILE), 0)

    def spread(a, b, c, low):
        picked = jnp.where(eight == low, a, 0.0)
        picked = jnp.where(eight == low + 1, b, picked)
        picked = jnp.where(eight == low + 2, c, picked)
        other = 3 - low
        return jnp.where((eight >= other) & (eight < other + 3), 1.0, picked)

    def prepare(tile, data):
        mid, vector = data[0:8], data[8:16]
        m1, m2, m3 = pieces_of(mid)
        b1, b2, b3 = pieces_of(vector)
        norm = jnp.sum(mid * mid, axis=0, keepdims=True)
        none = jnp.zeros((8, TILE), f32)
        left_norm = spread(*pieces_of(norm + core_square), 0)
        right_norm = spread(*pieces_of(norm), 3)
        left = [-2.0 * m1, -2.0 * m1, -2.0 * m2, -2.0 * m2, -2.0 * m1, -2.0 * m3, left_norm]
        left += [near_scale * b for b in (b1, b1, b2, b2, b1, b3)] + [none] * 3
        left_ops[tile] = jnp.concatenate(left, axis=0).T.astype(bf16)
        far_half = jnp.concatenate([m1, m2, m1, m2, m3, m1, right_norm] + [none] * 9, axis=0)
        dot_half = jnp.concatenate([none] * 7 + [b1, b2, b1, b2, b3, b1] + [none] * 3, axis=0)
        right_ops[tile, :, 0:TILE] = far_half.astype(bf16)
        right_ops[tile, :, TILE : 2 * TILE] = dot_half.astype(bf16)
        mids = jnp.concatenate([m1, m2, m3, jnp.ones((8, TILE), f32)], axis=0).astype(bf16)
        mid_ops[tile, :, 0:TILE] = mids
        mid_ops[tile, :, TILE : 2 * TILE] = mids

    @pl.loop(0, local_tiles // 4)
    def _(step):
        for k in range(4):
            prepare(step * 4 + k, raw[step * 4 + k])

    for n in range(4):
        ghost_copies[n].wait()
        data = ghost_in[n]
        raw[local_tiles + n] = data
        prepare(local_tiles + n, data)

    def pairs(step):
        base = step * TOGETHER
        targets = [jnp.maximum(pair_smem[0, base + k], 0) for k in range(TOGETHER)]
        sources = [jnp.maximum(pair_smem[1, base + k], 0) for k in range(TOGETHER)]
        both = [dot(left_ops[targets[k]], right_ops[sources[k]]) for k in range(TOGETHER)]
        for k in range(TOGETHER):
            near = lax.rsqrt(both[k][:, 0:TILE])
            weight = both[k][:, TILE : 2 * TILE] * (near * near * near)
            coarse = weight.astype(bf16)
            fine = (weight - coarse.astype(f32)).astype(bf16)
            on_target = dot(mid_ops[sources[k]], jnp.concatenate([coarse, fine], axis=1), NT)
            on_source = dot(mid_ops[targets[k]], jnp.concatenate([coarse, fine], axis=0))
            for side, tile, got in ((0, targets[k], on_target), (1, sources[k], on_source)):
                force = raw[tile][0:8] * got[24:32] - (got[0:8] + got[8:16] + got[16:24])
                for c in range(3):
                    pushed[c, pl.ds(side * pair_count + base + k, 1)] = force[c : c + 1]

    steps = pair_count // TOGETHER
    pl.loop(0, steps // 2)(pairs)

    for copy in column_copies:
        copy.wait()
    along = dot_high(column_slots[0], column_ref[0])
    for slot in range(1, column_count):
        along = along + dot_high(column_slots[slot], column_ref[slot])
    slab_slots[0] = along
    slab_copies = []
    for by in range(1, slab_count):
        copy = pltpu.make_async_remote_copy(
            src_ref=slab_slots.at[0],
            dst_ref=slab_slots.at[slab_count - by],
            send_sem=slab_send.at[by],
            recv_sem=slab_recv.at[slab_count - by],
            device_id=slab_peer(by),
            device_id_type=MESH,
        )
        copy.start()
        slab_copies.append(copy)

    pl.loop(steps // 2, steps)(pairs)

    tile_rows = -(-(local_tiles + 4) // 16) * 16
    ids = lax.broadcasted_iota(jnp.int32, (tile_rows, pair_count), 0)
    targets = pair_ref[0:1, :]
    sources = pair_ref[1:2, :]
    to_target = jnp.where(ids == targets, 1.0, 0.0)
    to_source = jnp.where((ids == sources) & (targets != sources), 1.0, 0.0)
    to_tile = jnp.concatenate([to_target, to_source], axis=1).astype(bf16)
    near = []
    for c in range(3):
        first, second, third = (piece.astype(bf16) for piece in pieces_of(pushed[c]))
        near.append(dot(to_tile, first) + dot(to_tile, second) + dot(to_tile, third))
    return_out[...] = jnp.zeros_like(return_out)
    return_copies = []
    for n in range(4):
        for c in range(3):
            return_out[n, c : c + 1] = near[c][local_tiles + n : local_tiles + n + 1]
        copy = pltpu.make_async_remote_copy(
            src_ref=return_out.at[n],
            dst_ref=return_in.at[n],
            send_sem=return_send.at[n],
            recv_sem=return_recv.at[n],
            device_id=backward[n],
            device_id_type=MESH,
        )
        copy.start()
        return_copies.append(copy)

    for copy in slab_copies:
        copy.wait()
    along = dot_high(slab_ref[0], slab_slots[0])
    for slot in range(1, slab_count):
        along = along + dot_high(slab_ref[slot], slab_slots[slot])
    stress[...] = jnp.concatenate([piece.astype(bf16) for piece in pieces_of(along)], axis=0)

    @pl.loop(0, seg_count // CHUNK)
    def _(step):
        at = pl.ds(pl.multiple_of(step * CHUNK, CHUNK), CHUNK)
        high = cell_ref[:, at] // cells
        count = span_x * 8
        got = dot(stress[...], hot_cells[:, at])
        got = got[0:count] + got[count : 2 * count] + got[2 * count : 3 * count]
        s = jnp.zeros((8, CHUNK), f32)
        for x in range(span_x):
            s = s + jnp.where(high == x, got[x * 8 : (x + 1) * 8], 0.0)
        t = seg_ref[3:6, at] - seg_ref[0:3, at]
        b = burgers_ref[:, at]
        push_x = s[0:1] * b[0:1] + s[5:6] * b[1:2] + s[4:5] * b[2:3]
        push_y = s[5:6] * b[0:1] + s[1:2] * b[1:2] + s[3:4] * b[2:3]
        push_z = s[4:5] * b[0:1] + s[3:4] * b[1:2] + s[2:3] * b[2:3]
        out_ref[0:1, at] = push_y * t[2:3] - push_z * t[1:2]
        out_ref[1:2, at] = push_z * t[0:1] - push_x * t[2:3]
        out_ref[2:3, at] = push_x * t[1:2] - push_y * t[0:1]

    for copy in return_copies:
        copy.wait()
    returned = jnp.concatenate([return_in[n] for n in range(4)], axis=1)
    back = None
    for piece in pieces_of(returned):
        parts = [jnp.where(row_tile == tile, piece, 0.0) for tile in range(local_tiles)]
        term = dot(jnp.concatenate(parts, axis=0).astype(bf16), hot_rows, NT)
        back = term if back is None else back + term
    for tile in range(local_tiles):
        at = slice(tile * TILE, (tile + 1) * TILE)
        for c in range(3):
            out_ref[c : c + 1, at] += (
                near[c][tile : tile + 1] + back[tile * 8 + c : tile * 8 + c + 1]
            )


def on_device(seg_ends, burgers, cell_index, send_list, pair_list, coupling):
    slab_count = lax.axis_size("gx")
    column_count = lax.axis_size("yz")
    span_x = G // slab_count
    span_y = G // column_count
    seg_count = seg_ends.shape[1]
    tiles = seg_count // TILE + 4
    columns = jnp.asarray(column_matrices(column_count, span_y))
    slabs = jnp.asarray(slab_matrices(slab_count, span_x))
    width = columns.shape[1]
    vmem = pl.BlockSpec(memory_space=pltpu.VMEM)
    smem = pl.BlockSpec(memory_space=pltpu.SMEM)
    sems = pltpu.SemaphoreType.DMA
    return pl.pallas_call(
        functools.partial(body, span_x, span_y, slab_count, column_count),
        out_shape=jax.ShapeDtypeStruct((3, seg_count), f32),
        in_specs=[vmem] * 5 + [smem] + [vmem] * 3,
        out_specs=vmem,
        scratch_shapes=[
            pltpu.VMEM((tiles - 4 + 4, 16, TILE), f32),
            pltpu.VMEM((4, 16, TILE), f32),
            pltpu.VMEM((4, 16, TILE), f32),
            pltpu.VMEM((tiles, TILE, TILE), bf16),
            pltpu.VMEM((tiles, TILE, 2 * TILE), bf16),
            pltpu.VMEM((tiles, 32, 2 * TILE), bf16),
            pltpu.VMEM((width, seg_count), bf16),
            pltpu.VMEM((3 * span_x * 16, width), f32),
            pltpu.VMEM((column_count, span_x * 8, width), f32),
            pltpu.VMEM((slab_count, span_x * 8, width), f32),
            pltpu.VMEM((3 * span_x * 8, width), bf16),
            pltpu.VMEM((3, 2 * pair_list.shape[1], TILE), f32),
            pltpu.VMEM((4, 8, TILE), f32),
            pltpu.VMEM((4, 8, TILE), f32),
            sems((4,)),
            sems((4,)),
            sems((column_count,)),
            sems((column_count,)),
            sems((slab_count,)),
            sems((slab_count,)),
            sems((4,)),
            sems((4,)),
        ],
        compiler_params=pltpu.CompilerParams(
            collective_id=0, has_side_effects=True, vmem_limit_bytes=40 * 1024 * 1024
        ),
        name="dislocation_forces",
    )(
        seg_ends,
        burgers,
        cell_index.reshape(1, seg_count),
        send_list,
        pair_list,
        pair_list,
        coupling,
        columns,
        slabs,
    )


def solution(mesh):
    placed = (
        P(None, ("gx", "yz")),
        P(None, ("gx", "yz")),
        P(("gx", "yz")),
        P(None, ("gx", "yz")),
        P(None, ("gx", "yz")),
        P(),
    )
    return jax.shard_map(
        on_device, mesh=mesh, in_specs=placed, out_specs=P(None, ("gx", "yz")), check_vma=False
    )
```

```python
import functools

import jax
import jax.numpy as jnp
import numpy as np
from jax import lax
from jax.experimental import pallas as pl
from jax.experimental.pallas import tpu as pltpu
from jax.sharding import PartitionSpec as P

G = 32
TILE = 128
LANES = 128
TOGETHER = 8
CHUNK = 512

far_scale = 0.003
near_scale = 0.25
core_square = 1.0
kernel_spread = 4.0

MESH = pl.DeviceIdType.MESH
f32 = jnp.float32
bf16 = jnp.bfloat16
NT = (((1,), (1,)), ((), ()))
NN = (((1,), (0,)), ((), ()))


def kernel_of(apart):
    apart = np.abs(apart) % G
    apart = np.minimum(apart, G - apart).astype(np.float32)
    return (1.0 / (1.0 + (apart / np.float32(kernel_spread)) ** 2)).astype(np.float32)


def column_matrices(column_count, span_y):
    cells = span_y * G
    width = -(-cells // LANES) * LANES
    at = np.arange(cells)
    result = np.zeros((column_count, width, width), np.float32)
    for slot in range(column_count):
        from_y = slot * span_y + at // G
        result[slot, :cells, :cells] = kernel_of(from_y[:, None] - (at // G)[None, :]) * kernel_of(
            (at % G)[:, None] - (at % G)[None, :]
        )
    return result


def slab_matrices(slab_count, span_x):
    at = np.arange(span_x)
    result = []
    for slot in range(slab_count):
        along = kernel_of((slot * span_x + at)[None, :] - at[:, None]) * np.float32(far_scale)
        result.append(np.kron(along, np.eye(8, dtype=np.float32)))
    return np.stack(result).astype(np.float32)


def pieces_of(x):
    first = x.astype(bf16).astype(f32)
    rest = x - first
    second = rest.astype(bf16).astype(f32)
    return first, second, rest - second


def dot(a, b, dims=NN):
    return lax.dot_general(a, b, dims, preferred_element_type=f32)


def dot_high(a, b):
    return lax.dot_general(a, b, NN, precision=lax.Precision.HIGHEST, preferred_element_type=f32)


def body(
    span_x,
    span_y,
    slab_count,
    column_count,
    seg_hbm,
    burgers_hbm,
    cell_hbm,
    send_hbm,
    pair_hbm,
    coupling_hbm,
    column_hbm,
    slab_hbm,
    out_ref,
    seg_ref,
    burgers_ref,
    cell_ref,
    send_ref,
    pair_ref,
    pair_smem,
    coupling_ref,
    column_ref,
    slab_ref,
    raw,
    ghost_out,
    ghost_in,
    left_ops,
    right_ops,
    mid_ops,
    hot_cells,
    moments,
    column_slots,
    slab_slots,
    stress,
    pushed,
    return_out,
    return_in,
    ghost_send,
    ghost_recv,
    column_send,
    column_recv,
    slab_send,
    slab_recv,
    return_send,
    return_recv,
    load_sem,
):
    seg_count = seg_ref.shape[1]
    local_tiles = seg_count // TILE
    pair_count = pair_ref.shape[1]
    cells = span_y * G
    width = column_ref.shape[1]
    gx = lax.axis_index("gx")
    yz = lax.axis_index("yz")

    def slab_peer(by):
        return (lax.rem(gx + by, slab_count), yz)

    def column_peer(by):
        return (gx, lax.rem(yz + by, column_count))

    loads = []
    for source, destination in (
        (seg_hbm, seg_ref),
        (burgers_hbm, burgers_ref),
        (send_hbm, send_ref),
        (cell_hbm, cell_ref),
        (coupling_hbm, coupling_ref),
        (pair_hbm, pair_smem),
        (pair_hbm, pair_ref),
        (column_hbm, column_ref),
        (slab_hbm, slab_ref),
    ):
        load = pltpu.make_async_copy(source, destination, load_sem.at[len(loads)])
        load.start()
        loads.append(load)

    barrier = pltpu.get_barrier_semaphore()
    for by in range(1, slab_count):
        pl.semaphore_signal(barrier, inc=1, device_id=slab_peer(by), device_id_type=MESH)
    for by in range(1, column_count):
        pl.semaphore_signal(barrier, inc=1, device_id=column_peer(by), device_id_type=MESH)

    raw[...] = jnp.zeros_like(raw)
    for load in loads[0:3]:
        load.wait()
    for tile in range(local_tiles):
        at = slice(tile * TILE, (tile + 1) * TILE)
        raw[tile, 0:3] = 0.5 * (seg_ref[0:3, at] + seg_ref[3:6, at])
        raw[tile, 8:11] = burgers_ref[0:3, at]

    sub = lax.broadcasted_iota(jnp.int32, (TILE, 4 * TILE), 0)
    rows = jnp.concatenate([send_ref[n : n + 1, :] for n in range(4)], axis=1)
    row_tile = rows >> 7
    hot_rows = jnp.where(sub == (rows & 127), 1.0, 0.0).astype(bf16)
    flat = raw[0:local_tiles].reshape(local_tiles * 16, TILE)
    first, second, third = (piece.astype(bf16) for piece in pieces_of(flat))
    picked = dot(first, hot_rows) + dot(second, hot_rows) + dot(third, hot_rows)
    outgoing = jnp.zeros((16, 4 * TILE), f32)
    for tile in range(local_tiles):
        outgoing = outgoing + jnp.where(row_tile == tile, picked[tile * 16 : (tile + 1) * 16], 0.0)
    for n in range(4):
        ghost_out[n] = outgoing[:, n * TILE : (n + 1) * TILE]

    pl.semaphore_wait(barrier, slab_count - 1 + column_count - 1)

    onward = [
        slab_peer(1),
        slab_peer(slab_count - 1),
        column_peer(1),
        column_peer(column_count - 1),
    ]
    backward = [onward[1], onward[0], onward[3], onward[2]]
    ghost_copies = []
    for n in range(4):
        copy = pltpu.make_async_remote_copy(
            src_ref=ghost_out.at[n],
            dst_ref=ghost_in.at[n],
            send_sem=ghost_send.at[n],
            recv_sem=ghost_recv.at[n],
            device_id=onward[n],
            device_id_type=MESH,
        )
        copy.start()
        ghost_copies.append(copy)

    moments[...] = jnp.zeros_like(moments)
    for load in loads[3:5]:
        load.wait()

    @pl.loop(0, seg_count // CHUNK)
    def _(step):
        at = pl.ds(pl.multiple_of(step * CHUNK, CHUNK), CHUNK)
        cell = cell_ref[:, at]
        high = cell // cells
        low = cell - high * cells
        hot = jnp.where(lax.broadcasted_iota(jnp.int32, (width, CHUNK), 0) == low, 1.0, 0.0).astype(bf16)
        hot_cells[:, at] = hot
        tangent = seg_ref[3:6, at] - seg_ref[0:3, at]
        vector = burgers_ref[:, at]
        terms = jnp.concatenate(
            [vector[a : a + 1] * tangent for a in range(3)] + [jnp.zeros((7, CHUNK), f32)], axis=0
        )
        stacked = []
        for piece in pieces_of(terms):
            for x in range(span_x):
                stacked.append(jnp.where(high == x, piece, 0.0).astype(bf16))
        moments[...] += dot(jnp.concatenate(stacked, axis=0), hot, NT)

    count = span_x * 16
    summed = moments[0:count] + moments[count : 2 * count] + moments[2 * count : 3 * count]
    column_slots[0] = jnp.zeros_like(column_slots[0])
    for x in range(span_x):
        total = jnp.zeros((6, width), f32)
        for k in range(9):
            total = total + coupling_ref[:, k : k + 1] * summed[x * 16 + k : x * 16 + k + 1]
        column_slots[0, x * 8 : x * 8 + 6] = total

    column_copies = []
    for by in range(1, column_count):
        copy = pltpu.make_async_remote_copy(
            src_ref=column_slots.at[0],
            dst_ref=column_slots.at[column_count - by],
            send_sem=column_send.at[by],
            recv_sem=column_recv.at[column_count - by],
            device_id=column_peer(by),
            device_id_type=MESH,
        )
        copy.start()
        column_copies.append(copy)

    eight = lax.broadcasted_iota(jnp.int32, (8, TILE), 0)

    def spread(a, b, c, low):
        picked = jnp.where(eight == low, a, 0.0)
        picked = jnp.where(eight == low + 1, b, picked)
        picked = jnp.where(eight == low + 2, c, picked)
        other = 3 - low
        return jnp.where((eight >= other) & (eight < other + 3), 1.0, picked)

    def prepare(tile, data):
        mid, vector = data[0:8], data[8:16]
        m1, m2, m3 = pieces_of(mid)
        b1, b2, b3 = pieces_of(vector)
        norm = jnp.sum(mid * mid, axis=0, keepdims=True)
        none = jnp.zeros((8, TILE), f32)
        left_norm = spread(*pieces_of(norm + core_square), 0)
        right_norm = spread(*pieces_of(norm), 3)
        left = [-2.0 * m1, -2.0 * m1, -2.0 * m2, -2.0 * m2, -2.0 * m1, -2.0 * m3, left_norm]
        left += [near_scale * b for b in (b1, b1, b2, b2, b1, b3)] + [none] * 3
        left_ops[tile] = jnp.concatenate(left, axis=0).T.astype(bf16)
        far_half = jnp.concatenate([m1, m2, m1, m2, m3, m1, right_norm] + [none] * 9, axis=0)
        dot_half = jnp.concatenate([none] * 7 + [b1, b2, b1, b2, b3, b1] + [none] * 3, axis=0)
        right_ops[tile, :, 0:TILE] = far_half.astype(bf16)
        right_ops[tile, :, TILE : 2 * TILE] = dot_half.astype(bf16)
        mids = jnp.concatenate([m1, m2, m3, jnp.ones((8, TILE), f32)], axis=0).astype(bf16)
        mid_ops[tile, :, 0:TILE] = mids
        mid_ops[tile, :, TILE : 2 * TILE] = mids

    @pl.loop(0, local_tiles // 4)
    def _(step):
        for k in range(4):
            prepare(step * 4 + k, raw[step * 4 + k])

    for n in range(4):
        ghost_copies[n].wait()
        data = ghost_in[n]
        raw[local_tiles + n] = data
        prepare(local_tiles + n, data)

    def pairs(step):
        base = step * TOGETHER
        targets = [jnp.maximum(pair_smem[0, base + k], 0) for k in range(TOGETHER)]
        sources = [jnp.maximum(pair_smem[1, base + k], 0) for k in range(TOGETHER)]
        both = [dot(left_ops[targets[k]], right_ops[sources[k]]) for k in range(TOGETHER)]
        for k in range(TOGETHER):
            near = lax.rsqrt(both[k][:, 0:TILE])
            weight = both[k][:, TILE : 2 * TILE] * (near * near * near)
            coarse = weight.astype(bf16)
            fine = (weight - coarse.astype(f32)).astype(bf16)
            on_target = dot(mid_ops[sources[k]], jnp.concatenate([coarse, fine], axis=1), NT)
            on_source = dot(mid_ops[targets[k]], jnp.concatenate([coarse, fine], axis=0))
            for side, tile, got in ((0, targets[k], on_target), (1, sources[k], on_source)):
                force = raw[tile][0:8] * got[24:32] - (got[0:8] + got[8:16] + got[16:24])
                for c in range(3):
                    pushed[c, pl.ds(side * pair_count + base + k, 1)] = force[c : c + 1]

    for load in loads[5:9]:
        load.wait()
    steps = pair_count // TOGETHER
    pl.loop(0, steps // 2)(pairs)

    for copy in column_copies:
        copy.wait()
    along = dot_high(column_slots[0], column_ref[0])
    for slot in range(1, column_count):
        along = along + dot_high(column_slots[slot], column_ref[slot])
    slab_slots[0] = along
    slab_copies = []
    for by in range(1, slab_count):
        copy = pltpu.make_async_remote_copy(
            src_ref=slab_slots.at[0],
            dst_ref=slab_slots.at[slab_count - by],
            send_sem=slab_send.at[by],
            recv_sem=slab_recv.at[slab_count - by],
            device_id=slab_peer(by),
            device_id_type=MESH,
        )
        copy.start()
        slab_copies.append(copy)

    pl.loop(steps // 2, steps)(pairs)

    tile_rows = -(-(local_tiles + 4) // 16) * 16
    ids = lax.broadcasted_iota(jnp.int32, (tile_rows, pair_count), 0)
    targets = pair_ref[0:1, :]
    sources = pair_ref[1:2, :]
    to_target = jnp.where(ids == targets, 1.0, 0.0)
    to_source = jnp.where((ids == sources) & (targets != sources), 1.0, 0.0)
    to_tile = jnp.concatenate([to_target, to_source], axis=1).astype(bf16)
    near = []
    for c in range(3):
        first, second, third = (piece.astype(bf16) for piece in pieces_of(pushed[c]))
        near.append(dot(to_tile, first) + dot(to_tile, second) + dot(to_tile, third))
    return_out[...] = jnp.zeros_like(return_out)
    return_copies = []
    for n in range(4):
        for c in range(3):
            return_out[n, c : c + 1] = near[c][local_tiles + n : local_tiles + n + 1]
        copy = pltpu.make_async_remote_copy(
            src_ref=return_out.at[n],
            dst_ref=return_in.at[n],
            send_sem=return_send.at[n],
            recv_sem=return_recv.at[n],
            device_id=backward[n],
            device_id_type=MESH,
        )
        copy.start()
        return_copies.append(copy)

    for copy in slab_copies:
        copy.wait()
    along = dot_high(slab_ref[0], slab_slots[0])
    for slot in range(1, slab_count):
        along = along + dot_high(slab_ref[slot], slab_slots[slot])
    stress[...] = jnp.concatenate([piece.astype(bf16) for piece in pieces_of(along)], axis=0)

    @pl.loop(0, seg_count // CHUNK)
    def _(step):
        at = pl.ds(pl.multiple_of(step * CHUNK, CHUNK), CHUNK)
        high = cell_ref[:, at] // cells
        count = span_x * 8
        got = dot(stress[...], hot_cells[:, at])
        got = got[0:count] + got[count : 2 * count] + got[2 * count : 3 * count]
        s = jnp.zeros((8, CHUNK), f32)
        for x in range(span_x):
            s = s + jnp.where(high == x, got[x * 8 : (x + 1) * 8], 0.0)
        t = seg_ref[3:6, at] - seg_ref[0:3, at]
        b = burgers_ref[:, at]
        push_x = s[0:1] * b[0:1] + s[5:6] * b[1:2] + s[4:5] * b[2:3]
        push_y = s[5:6] * b[0:1] + s[1:2] * b[1:2] + s[3:4] * b[2:3]
        push_z = s[4:5] * b[0:1] + s[3:4] * b[1:2] + s[2:3] * b[2:3]
        out_ref[0:1, at] = push_y * t[2:3] - push_z * t[1:2]
        out_ref[1:2, at] = push_z * t[0:1] - push_x * t[2:3]
        out_ref[2:3, at] = push_x * t[1:2] - push_y * t[0:1]

    for copy in return_copies:
        copy.wait()
    returned = jnp.concatenate([return_in[n] for n in range(4)], axis=1)
    back = None
    for piece in pieces_of(returned):
        parts = [jnp.where(row_tile == tile, piece, 0.0) for tile in range(local_tiles)]
        term = dot(jnp.concatenate(parts, axis=0).astype(bf16), hot_rows, NT)
        back = term if back is None else back + term
    for tile in range(local_tiles):
        at = slice(tile * TILE, (tile + 1) * TILE)
        for c in range(3):
            out_ref[c : c + 1, at] += (
                near[c][tile : tile + 1] + back[tile * 8 + c : tile * 8 + c + 1]
            )


def on_device(seg_ends, burgers, cell_index, send_list, pair_list, coupling):
    slab_count = lax.axis_size("gx")
    column_count = lax.axis_size("yz")
    span_x = G // slab_count
    span_y = G // column_count
    seg_count = seg_ends.shape[1]
    tiles = seg_count // TILE + 4
    columns = jnp.asarray(column_matrices(column_count, span_y))
    slabs = jnp.asarray(slab_matrices(slab_count, span_x))
    width = columns.shape[1]
    vmem = pl.BlockSpec(memory_space=pltpu.VMEM)
    sems = pltpu.SemaphoreType.DMA
    return pl.pallas_call(
        functools.partial(body, span_x, span_y, slab_count, column_count),
        out_shape=jax.ShapeDtypeStruct((3, seg_count), f32),
        in_specs=[pl.BlockSpec(memory_space=pltpu.HBM)] * 8,
        out_specs=vmem,
        scratch_shapes=[
            pltpu.VMEM(seg_ends.shape, f32),
            pltpu.VMEM(burgers.shape, f32),
            pltpu.VMEM((1, seg_count), jnp.int32),
            pltpu.VMEM(send_list.shape, jnp.int32),
            pltpu.VMEM(pair_list.shape, jnp.int32),
            pltpu.SMEM(pair_list.shape, jnp.int32),
            pltpu.VMEM(coupling.shape, f32),
            pltpu.VMEM(columns.shape, f32),
            pltpu.VMEM(slabs.shape, f32),
            pltpu.VMEM((tiles - 4 + 4, 16, TILE), f32),
            pltpu.VMEM((4, 16, TILE), f32),
            pltpu.VMEM((4, 16, TILE), f32),
            pltpu.VMEM((tiles, TILE, TILE), bf16),
            pltpu.VMEM((tiles, TILE, 2 * TILE), bf16),
            pltpu.VMEM((tiles, 32, 2 * TILE), bf16),
            pltpu.VMEM((width, seg_count), bf16),
            pltpu.VMEM((3 * span_x * 16, width), f32),
            pltpu.VMEM((column_count, span_x * 8, width), f32),
            pltpu.VMEM((slab_count, span_x * 8, width), f32),
            pltpu.VMEM((3 * span_x * 8, width), bf16),
            pltpu.VMEM((3, 2 * pair_list.shape[1], TILE), f32),
            pltpu.VMEM((4, 8, TILE), f32),
            pltpu.VMEM((4, 8, TILE), f32),
            sems((4,)),
            sems((4,)),
            sems((column_count,)),
            sems((column_count,)),
            sems((slab_count,)),
            sems((slab_count,)),
            sems((4,)),
            sems((4,)),
            sems((9,)),
        ],
        compiler_params=pltpu.CompilerParams(
            collective_id=0, has_side_effects=True, vmem_limit_bytes=64 * 1024 * 1024
        ),
        name="dislocation_forces",
    )(
        seg_ends,
        burgers,
        cell_index.reshape(1, seg_count),
        send_list,
        pair_list,
        coupling,
        columns,
        slabs,
    )


def solution(mesh):
    placed = (
        P(None, ("gx", "yz")),
        P(None, ("gx", "yz")),
        P(("gx", "yz")),
        P(None, ("gx", "yz")),
        P(None, ("gx", "yz")),
        P(),
    )
    return jax.shard_map(
        on_device, mesh=mesh, in_specs=placed, out_specs=P(None, ("gx", "yz")), check_vma=False
    )
```
